256 devices in a mesh: site: 128 (over z, y, x_hi, core), sector: 2 (over x_lo).
Axes of the slice: x: 4 (x_hi: 2, x_lo: 2; x = x_hi * 2 + x_lo), y: 4, z: 8, core: 2. Of those that a mesh axis runs over, the one named last changes fastest.
Arguments:
- left_env: bfloat16 [128, 2, 30, 128, 128], P('site', 'sector'), may hold values from -6 to 6
- right_env: bfloat16 [128, 2, 30, 128, 128], P('site', 'sector'), may hold values from -6 to 6
- left_site: bfloat16 [128, 2, 4, 128, 128], P('site', 'sector'), may hold values from -0.5 to 0.5
- right_site: bfloat16 [128, 2, 4, 128, 128], P('site', 'sector'), may hold values from -0.5 to 0.5
- left_ket: int32 [128, 2, 30], P('site'), may hold values from 0 to 1
- right_ket: int32 [128, 2, 30], P('site'), may hold values from 0 to 1
- left_terms: int32 [128, 3, 2, 30, 16], P('site'), may hold values from 0 to 59, as said below
- right_terms: int32 [128, 3, 2, 30, 16], P('site'), may hold values from 0 to 59, as said below
- left_weight: float32 [128, 2, 30, 16], P('site'), may hold values from -2 to 2
- right_weight: float32 [128, 2, 30, 16], P('site'), may hold values from -2 to 2
- left_sizes: int32 [128, 2], P('site'), may hold values from 64 to 128
- right_sizes: int32 [128, 2], P('site'), may hold values from 64 to 128
Outputs:
- new_left: bfloat16 [128, 2, 30, 128, 128], P('site', 'sector')
- new_right: bfloat16 [128, 2, 30, 128, 128], P('site', 'sector')
The draws below stay inside these ranges and needn't reach their ends.
Inputs may be any that keep to these rules, and one draw needn't show every extreme that they name: `left_terms`: field 0 is an environment block index c * 30 + v; in term f of every output block, sector block c lies in owner f // (16 / 2), owners holding 1 block each. Field 1 is a local state below 4; field 2 a site block index a * 4 + s. `right_terms`: as for left_terms.
All inputs are finite; a program needn't handle non-finite values.
Results may differ from the reference program's by a relative error of at most 0.014.
Values may be sent and summed in bfloat16 or wider, within the bound.
A program may use at most 128 MiB of HBM per device.

```python
import jax
import jax.numpy as jnp
from jax import lax

P_SIZE = 128
W = 30
DPHYS = 4
F = 16
BLK_DEV = 1
KB = 2
GROUPS = 128
N_SECTOR = 2


def joining_draw(key):
    subkeys = jax.random.split(key, 4)
    per_owner = F // N_SECTOR
    owner_index = (jnp.arange(F) // per_owner)[None, None, None, :]
    local_block = jax.random.randint(subkeys[0], (GROUPS, KB, W, F), 0, BLK_DEV)
    column = jax.random.randint(subkeys[1], (GROUPS, KB, W, F), 0, W)
    env_index = (owner_index * BLK_DEV + local_block) * W + column
    physical = jax.random.randint(subkeys[2], (GROUPS, KB, W, F), 0, DPHYS)
    bra_index = jax.random.randint(subkeys[3], (GROUPS, KB, W, F), 0, KB * DPHYS)
    return jnp.stack([env_index, physical, bra_index], axis=1).astype(jnp.int32)


def draw_left_terms(key, part):
    key = jax.random.fold_in(key, 11)
    return joining_draw(key)


def draw_right_terms(key, part):
    key = jax.random.fold_in(key, 12)
    return joining_draw(key)


def plant(values, key, low, largest):
    index_at = [jax.random.randint(jax.random.fold_in(key, axis), (), 0, length) for axis, length in enumerate(values.shape)]
    longest = values.shape.index(max(values.shape))
    next_to = index_at[:longest] + [(index_at[longest] + 1) % values.shape[longest]] + index_at[longest + 1:]
    return values.at[tuple(index_at)].set(low).at[tuple(next_to)].set(largest)


def block_scale(rng, shape, cuts, smallest, high):
    loudness = 1.0
    for axis_at, shards_of in cuts:
        draws = jax.random.uniform(jax.random.fold_in(jax.random.fold_in(rng, 6), axis_at), (shards_of,), jnp.float32, smallest / len(cuts), high / len(cuts))
        loudness = loudness * jnp.repeat(jnp.exp(draws), shape[axis_at] // shards_of).reshape((-1,) + (1,) * (len(shape) - 1 - axis_at))
    return loudness


def normal_values(rng, dims, deviation, limit, cuts=(), dtype=jnp.bfloat16):
    result = deviation * jax.random.normal(rng, dims, jnp.float32)
    if cuts:
        result = result * block_scale(rng, dims, cuts, -0.22, 0.18)
    return jnp.clip(result, -limit, limit).astype(dtype)


def setup_inputs(seed: int = 0) -> dict:
    streams_of = jax.random.split(jax.random.key(seed), 13)
    return {
        "left_env": normal_values(streams_of[0], (GROUPS, KB, W, P_SIZE, P_SIZE), 1.0, 6.0, ((0, 128), (1, 2))),
        "right_env": normal_values(streams_of[1], (GROUPS, KB, W, P_SIZE, P_SIZE), 1.0, 6.0, ((0, 128), (1, 2))),
        "left_site": normal_values(streams_of[2], (GROUPS, KB, DPHYS, P_SIZE, P_SIZE), P_SIZE ** -0.5, 0.5, ((0, 128), (1, 2))),
        "right_site": normal_values(streams_of[3], (GROUPS, KB, DPHYS, P_SIZE, P_SIZE), P_SIZE ** -0.5, 0.5, ((0, 128), (1, 2))),
        "left_ket": plant(jax.random.randint(streams_of[4], (GROUPS, KB, W), 0, KB), jax.random.fold_in(streams_of[4], 1), 0, KB - 1).astype(jnp.int32),
        "right_ket": plant(jax.random.randint(streams_of[5], (GROUPS, KB, W), 0, KB), jax.random.fold_in(streams_of[5], 1), 0, KB - 1).astype(jnp.int32),
        "left_terms": draw_left_terms(jax.random.fold_in(streams_of[12], 71), 0),
        "right_terms": draw_right_terms(jax.random.fold_in(streams_of[12], 71), 0),
        "left_weight": normal_values(streams_of[8], (GROUPS, KB, W, F), 0.3, 2.0, ((0, 128),), jnp.float32),
        "right_weight": normal_values(streams_of[9], (GROUPS, KB, W, F), 0.3, 2.0, ((0, 128),), jnp.float32),
        "left_sizes": plant(jax.random.randint(streams_of[10], (GROUPS, KB), P_SIZE // 2, P_SIZE + 1), jax.random.fold_in(streams_of[10], 1), P_SIZE // 2, P_SIZE).astype(jnp.int32),
        "right_sizes": plant(jax.random.randint(streams_of[11], (GROUPS, KB), P_SIZE // 2, P_SIZE + 1), jax.random.fold_in(streams_of[11], 1), P_SIZE // 2, P_SIZE).astype(jnp.int32),
    }


def update_one(env, site, ket_table, term_rows, term_weight, sizes):
    flat_env = env.reshape(-1, P_SIZE, P_SIZE).astype(jnp.float32)
    row_mask = jnp.arange(P_SIZE)[None, None, :, None] < sizes[:, None, None, None]
    blocks = jnp.where(row_mask, site, jnp.zeros_like(site))
    ket_flat = ket_table.reshape(-1).astype(jnp.int32)

    def half_single(item):
        env_block, ket_index = item
        ket_take = blocks[ket_index].astype(jnp.float32)
        return jnp.einsum('pq,sqr->spr', env_block, ket_take).astype(jnp.bfloat16)

    half_table = lax.map(half_single, (flat_env, ket_flat))
    half_table = lax.optimization_barrier(half_table).reshape(-1, P_SIZE, P_SIZE)
    flat_blocks = blocks.reshape(-1, P_SIZE, P_SIZE)
    items = (term_rows[0].reshape(-1, F), term_rows[1].reshape(-1, F), term_rows[2].reshape(-1, F), term_weight.reshape(-1, F))

    def single(item):
        env_index, physical, bra_index, weights = item
        half_product = half_table[env_index * DPHYS + physical].astype(jnp.float32)
        bra_take = flat_blocks[bra_index].astype(jnp.float32)
        contribution = jnp.einsum('nqp,nqr->npr', bra_take, half_product)
        return jnp.sum(weights[:, None, None] * contribution, axis=0)

    return lax.map(single, items).reshape(KB, W, P_SIZE, P_SIZE).astype(jnp.bfloat16)


def update_all(env, site, ket_table, term_rows, term_weight, sizes):
    return lax.map(lambda item: update_one(*item), (env, site, ket_table, term_rows, term_weight, sizes))


def reference(left_env, right_env, left_site, right_site, left_ket, right_ket, left_terms, right_terms, left_weight, right_weight, left_sizes, right_sizes):
    left_update = update_all(left_env, left_site, left_ket, left_terms, left_weight, left_sizes)
    right_update = update_all(right_env, right_site, right_ket, right_terms, right_weight, right_sizes)
    new_left = jnp.concatenate([left_env[:1], left_update[:-1]], axis=0)
    new_right = jnp.concatenate([right_update[1:], right_env[-1:]], axis=0)
    return new_left, new_right
```

```python
import functools

import jax
import jax.numpy as jnp
from jax import lax
from jax.experimental import pallas as pl
from jax.experimental.pallas import tpu as pltpu
from jax.sharding import PartitionSpec as P

MESH = pl.DeviceIdType.MESH
CHUNK = 2
HALF_STEP = 2


def kernel(
    sites,
    left_env,
    right_env,
    left_site,
    right_site,
    left_ket,
    right_ket,
    left_terms,
    right_terms,
    left_weight,
    right_weight,
    left_sizes,
    right_sizes,
    out,
    env,
    site,
    ket,
    terms,
    weight,
    sizes,
    joined,
    bra,
    half,
    send,
    keep,
    recv,
    final,
    load_sem,
    site_send_sem,
    site_recv_sem,
    part_send_sem,
    part_recv_sem,
    out_send_sem,
    out_recv_sem,
    edge_sem,
):
    columns, width = env.shape[1], env.shape[2]
    degree = site.shape[2]
    term_count = terms.shape[3] // 2
    chunks = columns // CHUNK
    g, c = lax.axis_index("site"), lax.axis_index("sector")
    core = lax.rem(g, 2)
    other = 1 - c
    edge = (g == 0) | (g == sites - 1)
    mate = g + 1 - 2 * core
    far = lax.rem(g + 2 * core - 1 + sites, sites)

    loads = []
    for side, refs in enumerate(
        (
            (left_site, left_env, left_sizes, left_ket, left_terms, left_weight),
            (right_site, right_env, right_sizes, right_ket, right_terms, right_weight),
        )
    ):
        site_in, env_in, sizes_in, ket_in, terms_in, weight_in = refs
        for source, target in (
            (site_in.at[0, 0], site.at[side, c]),
            (env_in.at[0, 0], env.at[side]),
            (sizes_in.at[0], sizes.at[side]),
            (ket_in.at[0], ket.at[side]),
            (terms_in.at[0], terms.at[side]),
            (weight_in.at[0], weight.at[side]),
        ):
            loads.append(pltpu.make_async_copy(source, target, load_sem.at[len(loads)]))
    for load in loads:
        load.start()

    barrier = pltpu.get_barrier_semaphore()
    for peer in ((g, other), (mate, c), (far, other)):
        pl.semaphore_signal(barrier, inc=1, device_id=peer, device_id_type=MESH)
    pl.semaphore_wait(barrier, 3)
    per_side = len(loads) // 2
    loads[0].wait()
    loads[per_side].wait()

    def side_of(phase):
        return 1 - core if phase == 0 else core

    def site_copy(side, owner):
        return pltpu.make_async_remote_copy(
            src_ref=site.at[side, owner],
            dst_ref=site.at[side, owner],
            send_sem=site_send_sem.at[side],
            recv_sem=site_recv_sem.at[side],
            device_id=(g, other),
            device_id_type=MESH,
        )

    def part_copy(phase, chunk):
        blocks = pl.ds(chunk * CHUNK, CHUNK)
        return pltpu.make_async_remote_copy(
            src_ref=send.at[phase, blocks],
            dst_ref=recv.at[phase, blocks],
            send_sem=part_send_sem.at[phase, chunk],
            recv_sem=part_recv_sem.at[phase, chunk],
            device_id=(g, other),
            device_id_type=MESH,
        )

    def out_copy(phase, chunk, out_side):
        blocks = pl.ds(chunk * CHUNK, CHUNK)
        return pltpu.make_async_remote_copy(
            src_ref=final.at[phase, blocks],
            dst_ref=out.at[out_side, blocks],
            send_sem=out_send_sem.at[phase, chunk],
            recv_sem=out_recv_sem.at[phase, chunk],
            device_id=(far, other) if phase == 0 else (mate, c),
            device_id_type=MESH,
        )

    for phase in range(2):
        site_copy(side_of(phase), c).start()
    for side in range(2):
        for load in loads[side * per_side + 1 : (side + 1) * per_side]:
            load.wait()
    edge_copy = pltpu.make_async_copy(env.at[core], out.at[core], edge_sem)

    @pl.when(edge)
    def _():
        edge_copy.start()

    def prepare(side):
        site_copy(side, other).wait_recv()
        row = lax.broadcasted_iota(jnp.int32, (width, width), 0)

        def one(a, carry):
            inside = row < sizes[side, a]
            for s in range(degree):
                block = jnp.where(inside, site[side, a, s].astype(jnp.float32), 0.0)
                joined[side, a, :, s * width : (s + 1) * width] = block.astype(jnp.bfloat16)
                bra[side, a * degree + s] = block.T
            return carry

        lax.fori_loop(0, 2, one, 0)

        def step(i, carry):
            rows = []
            for b in range(HALF_STEP):
                v = i * HALF_STEP + b
                block = env[side, v]
                second = ket[side, c, v].astype(jnp.float32).astype(jnp.bfloat16)
                first = (1 - ket[side, c, v]).astype(jnp.float32).astype(jnp.bfloat16)
                rows.append(jnp.concatenate([block * first, block * second], axis=1))
            both = jnp.concatenate([joined[side, 0], joined[side, 1]], axis=0)
            table = jnp.dot(
                jnp.concatenate(rows, axis=0), both, preferred_element_type=jnp.float32
            ).astype(jnp.bfloat16)
            for b in range(HALF_STEP):
                for t in range(degree):
                    half[side, (i * HALF_STEP + b) * degree + t] = table[
                        b * width : (b + 1) * width, t * width : (t + 1) * width
                    ]
            return carry

        lax.fori_loop(0, columns // HALF_STEP, step, 0)

    def partial_sum(side, k, w):
        bras, halves = [], []
        for j in range(term_count):
            f = c * term_count + j
            v = jnp.maximum(terms[side, 0, k, f, w] - c * columns, 0)
            t = terms[side, 1, k, f, w]
            u = terms[side, 2, k, f, w]
            bras.append((bra[side, u] * weight[side, k, f, w]).astype(jnp.bfloat16))
            halves.append(half[side, v * degree + t])
        return jnp.dot(
            jnp.concatenate(bras, axis=1),
            jnp.concatenate(halves, axis=0),
            preferred_element_type=jnp.float32,
        )

    for phase in range(2):
        side = side_of(phase)
        prepare(side)
        sent_sector = c if phase == 0 else other

        def send_step(chunk, carry):
            for b in range(CHUNK):
                w = chunk * CHUNK + b
                send[phase, w] = partial_sum(side, sent_sector, w).astype(jnp.bfloat16)
            part_copy(phase, chunk).start()
            return carry

        lax.fori_loop(0, chunks, send_step, 0)

    for phase in range(2):
        side = side_of(phase)
        kept_sector = other if phase == 0 else c

        def keep_step(w, carry):
            keep[phase, w] = partial_sum(side, kept_sector, w)
            return carry

        lax.fori_loop(0, columns, keep_step, 0)

        def add_step(chunk, carry):
            part_copy(phase, chunk).wait_recv()
            for b in range(CHUNK):
                w = chunk * CHUNK + b
                total = keep[phase, w] + recv[phase, w].astype(jnp.float32)
                final[phase, w] = total.astype(jnp.bfloat16)
            copy = out_copy(phase, chunk, side)
            if phase == 0:

                @pl.when(jnp.logical_not(edge))
                def _():
                    copy.start()

            else:
                copy.start()
            return carry

        lax.fori_loop(0, chunks, add_step, 0)

    for phase in range(2):
        site_copy(side_of(phase), c).wait_send()

        def drain_step(chunk, carry):
            part_copy(phase, chunk).wait_send()
            copy = out_copy(phase, chunk, 1 - side_of(phase))
            if phase == 0:

                @pl.when(jnp.logical_not(edge))
                def _():
                    copy.wait()

            else:
                copy.wait()
            return carry

        lax.fori_loop(0, chunks, drain_step, 0)

    @pl.when(edge)
    def _():
        edge_copy.wait()


def on_device(*args):
    args = args[:6] + tuple(jnp.swapaxes(table, -1, -2) for table in args[6:10]) + args[10:]
    left_env, left_site, left_ket, left_terms = args[0], args[2], args[4], args[6]
    columns, width = left_env.shape[2], left_env.shape[3]
    degree = left_site.shape[2]
    chunks = columns // CHUNK
    blocks = (columns, width, width)
    bf16, f32 = jnp.bfloat16, jnp.float32
    sites = lax.axis_size("site")
    out = pl.pallas_call(
        functools.partial(kernel, sites),
        out_shape=jax.ShapeDtypeStruct((2,) + blocks, bf16),
        in_specs=[pl.BlockSpec(memory_space=pl.ANY)] * len(args),
        out_specs=pl.BlockSpec(memory_space=pl.ANY),
        scratch_shapes=[
            pltpu.VMEM((2,) + blocks, bf16),
            pltpu.VMEM((2, 2, degree, width, width), bf16),
            pltpu.SMEM((2,) + left_ket.shape[1:], jnp.int32),
            pltpu.SMEM((2,) + left_terms.shape[1:], jnp.int32),
            pltpu.SMEM((2,) + left_terms.shape[2:], f32),
            pltpu.SMEM((2, 2), jnp.int32),
            pltpu.VMEM((2, 2, width, degree * width), bf16),
            pltpu.VMEM((2, 2 * degree, width, width), f32),
            pltpu.VMEM((2, columns * degree, width, width), bf16),
            pltpu.VMEM((2,) + blocks, bf16),
            pltpu.VMEM((2,) + blocks, f32),
            pltpu.VMEM((2,) + blocks, bf16),
            pltpu.VMEM((2,) + blocks, bf16),
            pltpu.SemaphoreType.DMA((len(args),)),
            pltpu.SemaphoreType.DMA((2,)),
            pltpu.SemaphoreType.DMA((2,)),
            pltpu.SemaphoreType.DMA((2, chunks)),
            pltpu.SemaphoreType.DMA((2, chunks)),
            pltpu.SemaphoreType.DMA((2, chunks)),
            pltpu.SemaphoreType.DMA((2, chunks)),
            pltpu.SemaphoreType.DMA,
        ],
        compiler_params=pltpu.CompilerParams(
            collective_id=0, has_side_effects=True, vmem_limit_bytes=40 * 1024 * 1024
        ),
    )(*args)
    return out[0][None, None], out[1][None, None]


def solution(mesh):
    blocks = P("site", "sector", None, None, None)
    return jax.shard_map(
        on_device,
        mesh=mesh,
        in_specs=(
            blocks,
            blocks,
            blocks,
            blocks,
            P("site", None, None),
            P("site", None, None),
            P("site", None, None, None, None),
            P("site", None, None, None, None),
            P("site", None, None, None),
            P("site", None, None, None),
            P("site", None),
            P("site", None),
        ),
        out_specs=(blocks, blocks),
        check_vma=False,
    )
```

```python
import functools

import jax
import jax.numpy as jnp
from jax import lax
from jax.experimental import pallas as pl
from jax.experimental.pallas import tpu as pltpu
from jax.sharding import PartitionSpec as P

MESH = pl.DeviceIdType.MESH
CHUNK = 2
HALF_STEP = 2


def kernel(
    sites,
    left_env,
    right_env,
    left_site,
    right_site,
    left_ket,
    right_ket,
    left_terms,
    right_terms,
    left_weight,
    right_weight,
    left_sizes,
    right_sizes,
    out,
    env,
    site,
    ket,
    terms,
    weight,
    sizes,
    joined,
    bra,
    half,
    send,
    keep,
    recv,
    final,
    load_sem,
    site_send_sem,
    site_recv_sem,
    part_send_sem,
    part_recv_sem,
    out_send_sem,
    out_recv_sem,
    edge_sem,
):
    columns, width = env.shape[1], env.shape[2]
    degree = site.shape[2]
    term_count = terms.shape[3] // 2
    chunks = columns // CHUNK
    g, c = lax.axis_index("site"), lax.axis_index("sector")
    core = lax.rem(g, 2)
    other = 1 - c
    edge = (g == 0) | (g == sites - 1)
    mate = g + 1 - 2 * core
    far = lax.rem(g + 2 * core - 1 + sites, sites)

    loads = []
    for side, refs in enumerate(
        (
            (left_site, left_env, left_sizes, left_ket, left_terms, left_weight),
            (right_site, right_env, right_sizes, right_ket, right_terms, right_weight),
        )
    ):
        site_in, env_in, sizes_in, ket_in, terms_in, weight_in = refs
        for source, target in (
            (site_in.at[0, 0], site.at[side, c]),
            (env_in.at[0, 0], env.at[side]),
            (sizes_in.at[0], sizes.at[side]),
            (ket_in.at[0], ket.at[side]),
            (terms_in.at[0], terms.at[side]),
            (weight_in.at[0], weight.at[side]),
        ):
            loads.append(pltpu.make_async_copy(source, target, load_sem.at[len(loads)]))
    for load in loads:
        load.start()

    barrier = pltpu.get_barrier_semaphore()
    for peer in ((g, other), (mate, c), (far, other)):
        pl.semaphore_signal(barrier, inc=1, device_id=peer, device_id_type=MESH)
    pl.semaphore_wait(barrier, 3)
    per_side = len(loads) // 2
    loads[0].wait()
    loads[per_side].wait()

    def side_of(phase):
        return 1 - core if phase == 0 else core

    def site_copy(side, owner):
        return pltpu.make_async_remote_copy(
            src_ref=site.at[side, owner],
            dst_ref=site.at[side, owner],
            send_sem=site_send_sem.at[side],
            recv_sem=site_recv_sem.at[side],
            device_id=(g, other),
            device_id_type=MESH,
        )

    def part_copy(phase, chunk):
        blocks = pl.ds(chunk * CHUNK, CHUNK)
        return pltpu.make_async_remote_copy(
            src_ref=send.at[phase, blocks],
            dst_ref=recv.at[phase, blocks],
            send_sem=part_send_sem.at[phase, chunk],
            recv_sem=part_recv_sem.at[phase, chunk],
            device_id=(g, other),
            device_id_type=MESH,
        )

    def out_copy(phase, chunk, out_side):
        blocks = pl.ds(chunk * CHUNK, CHUNK)
        return pltpu.make_async_remote_copy(
            src_ref=final.at[phase, blocks],
            dst_ref=out.at[out_side, blocks],
            send_sem=out_send_sem.at[phase, chunk],
            recv_sem=out_recv_sem.at[phase, chunk],
            device_id=(far, other) if phase == 0 else (mate, c),
            device_id_type=MESH,
        )

    for phase in range(2):
        site_copy(side_of(phase), c).start()
    for side in range(2):
        for load in loads[side * per_side + 1 : (side + 1) * per_side]:
            load.wait()
    edge_copy = pltpu.make_async_copy(env.at[core], out.at[core], edge_sem)

    @pl.when(edge)
    def _():
        edge_copy.start()

    def prepare(side):
        site_copy(side, other).wait_recv()
        row = lax.broadcasted_iota(jnp.int32, (width, width), 0)

        def one(a, carry):
            inside = row < sizes[side, a]
            for s in range(degree):
                block = jnp.where(inside, site[side, a, s].astype(jnp.float32), 0.0)
                joined[side, a, :, s * width : (s + 1) * width] = block.astype(jnp.bfloat16)
                bra[side, a * degree + s] = block.T
            return carry

        lax.fori_loop(0, 2, one, 0)

        def step(i, carry):
            rows = []
            for b in range(HALF_STEP):
                v = i * HALF_STEP + b
                block = env[side, v]
                second = ket[side, c, v].astype(jnp.float32).astype(jnp.bfloat16)
                first = (1 - ket[side, c, v]).astype(jnp.float32).astype(jnp.bfloat16)
                rows.append(jnp.concatenate([block * first, block * second], axis=1))
            both = jnp.concatenate([joined[side, 0], joined[side, 1]], axis=0)
            table = jnp.dot(
                jnp.concatenate(rows, axis=0), both, preferred_element_type=jnp.float32
            ).astype(jnp.bfloat16)
            for b in range(HALF_STEP):
                for t in range(degree):
                    half[side, (i * HALF_STEP + b) * degree + t] = table[
                        b * width : (b + 1) * width, t * width : (t + 1) * width
                    ]
            return carry

        lax.fori_loop(0, columns // HALF_STEP, step, 0)

    def partial_sum(side, k, w):
        bras, halves = [], []
        for j in range(term_count):
            f = c * term_count + j
            v = jnp.maximum(terms[side, 0, k, f, w] - c * columns, 0)
            t = terms[side, 1, k, f, w]
            u = terms[side, 2, k, f, w]
            bras.append((bra[side, u] * weight[side, k, f, w]).astype(jnp.bfloat16))
            halves.append(half[side, v * degree + t])
        return jnp.dot(
            jnp.concatenate(bras, axis=1),
            jnp.concatenate(halves, axis=0),
            preferred_element_type=jnp.float32,
        )

    for phase in range(2):
        side = side_of(phase)
        prepare(side)
        sent_sector = c if phase == 0 else other

        def send_step(chunk, carry):
            for b in range(CHUNK):
                w = chunk * CHUNK + b
                send[phase, w] = partial_sum(side, sent_sector, w).astype(jnp.bfloat16)
            part_copy(phase, chunk).start()
            return carry

        lax.fori_loop(0, chunks, send_step, 0)

    for phase in range(2):
        side = side_of(phase)
        kept_sector = other if phase == 0 else c

        def keep_step(w, carry):
            keep[phase, w] = partial_sum(side, kept_sector, w)
            return carry

        lax.fori_loop(0, columns, keep_step, 0)

        def add_step(chunk, carry):
            part_copy(phase, chunk).wait_recv()
            for b in range(CHUNK):
                w = chunk * CHUNK + b
                total = keep[phase, w] + recv[phase, w].astype(jnp.float32)
                final[phase, w] = total.astype(jnp.bfloat16)
            copy = out_copy(phase, chunk, side)
            if phase == 0:

                @pl.when(jnp.logical_not(edge))
                def _():
                    copy.start()

            else:
                copy.start()
            return carry

        lax.fori_loop(0, chunks, add_step, 0)

    for phase in range(2):
        site_copy(side_of(phase), c).wait_send()

        def drain_step(chunk, carry):
            part_copy(phase, chunk).wait_send()
            copy = out_copy(phase, chunk, 1 - side_of(phase))
            if phase == 0:

                @pl.when(jnp.logical_not(edge))
                def _():
                    copy.wait()

            else:
                copy.wait()
            return carry

        lax.fori_loop(0, chunks, drain_step, 0)

    @pl.when(edge)
    def _():
        edge_copy.wait()


def on_device(*args):
    args = args[:6] + tuple(jnp.swapaxes(table, -1, -2) for table in args[6:10]) + args[10:]
    left_env, left_site, left_ket, left_terms = args[0], args[2], args[4], args[6]
    columns, width = left_env.shape[2], left_env.shape[3]
    degree = left_site.shape[2]
    chunks = columns // CHUNK
    blocks = (columns, width, width)
    bf16, f32 = jnp.bfloat16, jnp.float32
    sites = lax.axis_size("site")
    out = pl.pallas_call(
        functools.partial(kernel, sites),
        out_shape=jax.ShapeDtypeStruct((2,) + blocks, bf16),
        in_specs=[pl.BlockSpec(memory_space=pltpu.HBM)] * len(args),
        out_specs=pl.BlockSpec(memory_space=pl.ANY),
        scratch_shapes=[
            pltpu.VMEM((2,) + blocks, bf16),
            pltpu.VMEM((2, 2, degree, width, width), bf16),
            pltpu.SMEM((2,) + left_ket.shape[1:], jnp.int32),
            pltpu.SMEM((2,) + left_terms.shape[1:], jnp.int32),
            pltpu.SMEM((2,) + left_terms.shape[2:], f32),
            pltpu.SMEM((2, 2), jnp.int32),
            pltpu.VMEM((2, 2, width, degree * width), bf16),
            pltpu.VMEM((2, 2 * degree, width, width), f32),
            pltpu.VMEM((2, columns * degree, width, width), bf16),
            pltpu.VMEM((2,) + blocks, bf16),
            pltpu.VMEM((2,) + blocks, f32),
            pltpu.VMEM((2,) + blocks, bf16),
            pltpu.VMEM((2,) + blocks, bf16),
            pltpu.SemaphoreType.DMA((len(args),)),
            pltpu.SemaphoreType.DMA((2,)),
            pltpu.SemaphoreType.DMA((2,)),
            pltpu.SemaphoreType.DMA((2, chunks)),
            pltpu.SemaphoreType.DMA((2, chunks)),
            pltpu.SemaphoreType.DMA((2, chunks)),
            pltpu.SemaphoreType.DMA((2, chunks)),
            pltpu.SemaphoreType.DMA,
        ],
        compiler_params=pltpu.CompilerParams(
            collective_id=0, has_side_effects=True, vmem_limit_bytes=40 * 1024 * 1024
        ),
    )(*[pltpu.with_memory_space_constraint(a, pltpu.HBM) for a in args])
    return out[0][None, None], out[1][None, None]


def solution(mesh):
    blocks = P("site", "sector", None, None, None)
    return jax.shard_map(
        on_device,
        mesh=mesh,
        in_specs=(
            blocks,
            blocks,
            blocks,
            blocks,
            P("site", None, None),
            P("site", None, None),
            P("site", None, None, None, None),
            P("site", None, None, None, None),
            P("site", None, None, None),
            P("site", None, None, None),
            P("site", None),
            P("site", None),
        ),
        out_specs=(blocks, blocks),
        check_vma=False,
    )
```

```python
import functools

import jax
import jax.numpy as jnp
from jax import lax
from jax.experimental import pallas as pl
from jax.experimental.pallas import tpu as pltpu
from jax.sharding import PartitionSpec as P

MESH = pl.DeviceIdType.MESH
CHUNK = 2
HALF_STEP = 10


def kernel(
    sites,
    left_env,
    right_env,
    left_site,
    right_site,
    left_ket,
    right_ket,
    left_terms,
    right_terms,
    left_weight,
    right_weight,
    left_sizes,
    right_sizes,
    out,
    env,
    site,
    ket,
    terms,
    weight,
    sizes,
    joined,
    bra,
    half,
    send,
    keep,
    recv,
    mate_send,
    mate_recv,
    final,
    load_sem,
    site_send_sem,
    site_recv_sem,
    part_send_sem,
    part_recv_sem,
    mate_send_sem,
    mate_recv_sem,
    out_send_sem,
    out_recv_sem,
    edge_sem,
):
    columns, width = env.shape[1], env.shape[2]
    degree = site.shape[2]
    term_count = terms.shape[3] // 2
    chunks = columns // CHUNK
    g, c = lax.axis_index("site"), lax.axis_index("sector")
    core = lax.rem(g, 2)
    other = 1 - c
    inner = (g > 0) & (g < sites - 1)
    edge = jnp.logical_not(inner)
    mate = g + 1 - 2 * core
    far = lax.rem(g + 2 * core - 1 + sites, sites)

    loads = []
    for side, refs in enumerate(
        (
            (left_site, left_env, left_sizes, left_ket, left_terms, left_weight),
            (right_site, right_env, right_sizes, right_ket, right_terms, right_weight),
        )
    ):
        site_in, env_in, sizes_in, ket_in, terms_in, weight_in = refs
        for source, target in (
            (site_in.at[0, 0], site.at[side, c]),
            (env_in.at[0, 0], env.at[side]),
            (sizes_in.at[0], sizes.at[side]),
            (ket_in.at[0], ket.at[side]),
            (terms_in.at[0], terms.at[side]),
            (weight_in.at[0], weight.at[side]),
        ):
            loads.append(pltpu.make_async_copy(source, target, load_sem.at[len(loads)]))
    for load in loads:
        load.start()

    barrier = pltpu.get_barrier_semaphore()
    for peer in ((g, other), (mate, c), (mate, other)):
        pl.semaphore_signal(barrier, inc=1, device_id=peer, device_id_type=MESH)

    @pl.when(inner)
    def _():
        pl.semaphore_signal(barrier, inc=1, device_id=(far, other), device_id_type=MESH)

    pl.semaphore_wait(barrier, jnp.where(inner, 4, 3))
    per_side = len(loads) // 2
    loads[0].wait()
    loads[per_side].wait()

    def side_of(phase):
        return 1 - core if phase == 0 else core

    def site_copy(side, owner):
        return pltpu.make_async_remote_copy(
            src_ref=site.at[side, owner],
            dst_ref=site.at[side, owner],
            send_sem=site_send_sem.at[side],
            recv_sem=site_recv_sem.at[side],
            device_id=(g, other),
            device_id_type=MESH,
        )

    def chunk_copy(source, target, send_sems, recv_sems, chunk, device):
        blocks = pl.ds(chunk * CHUNK, CHUNK)
        return pltpu.make_async_remote_copy(
            src_ref=source.at[blocks],
            dst_ref=target.at[blocks],
            send_sem=send_sems.at[chunk],
            recv_sem=recv_sems.at[chunk],
            device_id=device,
            device_id_type=MESH,
        )

    def part_copy(phase, chunk):
        return chunk_copy(
            send.at[phase],
            recv.at[phase],
            part_send_sem.at[phase],
            part_recv_sem.at[phase],
            chunk,
            (g if phase == 0 else mate, other),
        )

    def mate_copy(chunk):
        return chunk_copy(mate_send, mate_recv, mate_send_sem, mate_recv_sem, chunk, (mate, c))

    def out_copy(chunk, side):
        return chunk_copy(final, out.at[side], out_send_sem, out_recv_sem, chunk, (far, other))

    for phase in range(2):
        site_copy(side_of(phase), c).start()
    for side in range(2):
        for load in loads[side * per_side + 1 : (side + 1) * per_side]:
            load.wait()
    edge_copy = pltpu.make_async_copy(env.at[core], out.at[core], edge_sem)

    @pl.when(edge)
    def _():
        edge_copy.start()

    row = lax.broadcasted_iota(jnp.int32, (width, width), 0)

    def prepare(side, a):
        inside = row < sizes[side, a]
        for s in range(degree):
            block = jnp.where(inside, site[side, a, s].astype(jnp.float32), 0.0)
            joined[side, a, :, s * width : (s + 1) * width] = block.astype(jnp.bfloat16)
            bra[side, a * degree + s] = block.T

    def fill_half(side):
        def step(i, carry):
            rows = []
            for b in range(HALF_STEP):
                v = i * HALF_STEP + b
                block = env[side, v]
                second = ket[side, c, v].astype(jnp.float32).astype(jnp.bfloat16)
                first = (1 - ket[side, c, v]).astype(jnp.float32).astype(jnp.bfloat16)
                rows.append(jnp.concatenate([block * first, block * second], axis=1))
            both = jnp.concatenate([joined[side, 0], joined[side, 1]], axis=0)
            table = jnp.dot(
                jnp.concatenate(rows, axis=0), both, preferred_element_type=jnp.float32
            ).astype(jnp.bfloat16)
            for b in range(HALF_STEP):
                for t in range(degree):
                    half[side, (i * HALF_STEP + b) * degree + t] = table[
                        b * width : (b + 1) * width, t * width : (t + 1) * width
                    ]
            return carry

        lax.fori_loop(0, columns // HALF_STEP, step, 0)

    def partial_sum(side, k, w):
        bras, halves = [], []
        for j in range(term_count):
            f = c * term_count + j
            v = jnp.maximum(terms[side, 0, k, f, w] - c * columns, 0)
            t = terms[side, 1, k, f, w]
            u = terms[side, 2, k, f, w]
            bras.append((bra[side, u] * weight[side, k, f, w]).astype(jnp.bfloat16))
            halves.append(half[side, v * degree + t])
        return jnp.dot(
            jnp.concatenate(bras, axis=1),
            jnp.concatenate(halves, axis=0),
            preferred_element_type=jnp.float32,
        )

    far_side, mate_side = side_of(0), side_of(1)

    def send_chunk(phase, chunk):
        for b in range(CHUNK):
            w = chunk * CHUNK + b
            sector = c if phase == 0 else other
            send[phase, w] = partial_sum(side_of(phase), sector, w).astype(jnp.bfloat16)
        part_copy(phase, chunk).start()

    def far_send_step(chunk, carry):
        send_chunk(0, chunk)
        return carry

    def far_keep_step(w, carry):
        keep[w] = partial_sum(far_side, other, w)
        return carry

    def mate_send_step(chunk, carry):
        send_chunk(1, chunk)
        part_copy(0, chunk).wait_recv()
        for b in range(CHUNK):
            w = chunk * CHUNK + b
            final[w] = (keep[w] + recv[0, w].astype(jnp.float32)).astype(jnp.bfloat16)

        @pl.when(inner)
        def _():
            out_copy(chunk, far_side).start()

        return carry

    def mate_keep_step(chunk, carry):
        for b in range(CHUNK):
            w = chunk * CHUNK + b
            mate_send[w] = partial_sum(mate_side, c, w).astype(jnp.bfloat16)
        mate_copy(chunk).start()
        return carry

    def mate_add_step(chunk, carry):
        mate_copy(chunk).wait_recv()
        part_copy(1, chunk).wait_recv()
        for b in range(CHUNK):
            w = chunk * CHUNK + b
            total = mate_recv[w].astype(jnp.float32) + recv[1, w].astype(jnp.float32)
            out[far_side, w] = total.astype(jnp.bfloat16)
        return carry

    def drain_step(chunk, carry):
        part_copy(0, chunk).wait_send()
        part_copy(1, chunk).wait_send()
        mate_copy(chunk).wait_send()

        @pl.when(inner)
        def _():
            out_copy(chunk, mate_side).wait()

        return carry

    prepare(far_side, c)
    prepare(mate_side, c)
    site_copy(far_side, other).wait_recv()
    prepare(far_side, other)
    fill_half(far_side)
    lax.fori_loop(0, chunks, far_send_step, 0)
    lax.fori_loop(0, columns, far_keep_step, 0)
    site_copy(mate_side, other).wait_recv()
    prepare(mate_side, other)
    fill_half(mate_side)
    lax.fori_loop(0, chunks, mate_send_step, 0)
    lax.fori_loop(0, chunks, mate_keep_step, 0)
    lax.fori_loop(0, chunks, mate_add_step, 0)
    for phase in range(2):
        site_copy(side_of(phase), c).wait_send()
    lax.fori_loop(0, chunks, drain_step, 0)

    @pl.when(edge)
    def _():
        edge_copy.wait()


def on_device(*args):
    args = args[:6] + tuple(jnp.swapaxes(table, -1, -2) for table in args[6:10]) + args[10:]
    left_env, left_site, left_ket, left_terms = args[0], args[2], args[4], args[6]
    columns, width = left_env.shape[2], left_env.shape[3]
    degree = left_site.shape[2]
    chunks = columns // CHUNK
    blocks = (columns, width, width)
    bf16, f32 = jnp.bfloat16, jnp.float32
    sites = lax.axis_size("site")
    out = pl.pallas_call(
        functools.partial(kernel, sites),
        out_shape=jax.ShapeDtypeStruct((2,) + blocks, bf16),
        in_specs=[pl.BlockSpec(memory_space=pltpu.HBM)] * len(args),
        out_specs=pl.BlockSpec(memory_space=pltpu.VMEM),
        scratch_shapes=[
            pltpu.VMEM((2,) + blocks, bf16),
            pltpu.VMEM((2, 2, degree, width, width), bf16),
            pltpu.SMEM((2,) + left_ket.shape[1:], jnp.int32),
            pltpu.SMEM((2,) + left_terms.shape[1:], jnp.int32),
            pltpu.SMEM((2,) + left_terms.shape[2:], f32),
            pltpu.SMEM((2, 2), jnp.int32),
            pltpu.VMEM((2, 2, width, degree * width), bf16),
            pltpu.VMEM((2, 2 * degree, width, width), f32),
            pltpu.VMEM((2, columns * degree, width, width), bf16),
            pltpu.VMEM((2,) + blocks, bf16),
            pltpu.VMEM(blocks, f32),
            pltpu.VMEM((2,) + blocks, bf16),
            pltpu.VMEM(blocks, bf16),
            pltpu.VMEM(blocks, bf16),
            pltpu.VMEM(blocks, bf16),
            pltpu.SemaphoreType.DMA((len(args),)),
            pltpu.SemaphoreType.DMA((2,)),
            pltpu.SemaphoreType.DMA((2,)),
            pltpu.SemaphoreType.DMA((2, chunks)),
            pltpu.SemaphoreType.DMA((2, chunks)),
            pltpu.SemaphoreType.DMA((chunks,)),
            pltpu.SemaphoreType.DMA((chunks,)),
            pltpu.SemaphoreType.DMA((chunks,)),
            pltpu.SemaphoreType.DMA((chunks,)),
            pltpu.SemaphoreType.DMA,
        ],
        compiler_params=pltpu.CompilerParams(
            collective_id=0, has_side_effects=True, vmem_limit_bytes=40 * 1024 * 1024
        ),
    )(*[pltpu.with_memory_space_constraint(a, pltpu.HBM) for a in args])
    return out[0][None, None], out[1][None, None]


def solution(mesh):
    blocks = P("site", "sector", None, None, None)
    return jax.shard_map(
        on_device,
        mesh=mesh,
        in_specs=(
            blocks,
            blocks,
            blocks,
            blocks,
            P("site", None, None),
            P("site", None, None),
            P("site", None, None, None, None),
            P("site", None, None, None, None),
            P("site", None, None, None),
            P("site", None, None, None),
            P("site", None),
            P("site", None),
        ),
        out_specs=(blocks, blocks),
        check_vma=False,
    )
```

```python
import functools

import jax
import jax.numpy as jnp
from jax import lax
from jax.experimental import pallas as pl
from jax.experimental.pallas import tpu as pltpu
from jax.sharding import PartitionSpec as P

MESH = pl.DeviceIdType.MESH
CHUNK = 5
HALF_STEP = 10


def kernel(
    sites,
    left_env,
    right_env,
    left_site,
    right_site,
    left_ket,
    right_ket,
    left_terms,
    right_terms,
    left_weight,
    right_weight,
    left_sizes,
    right_sizes,
    out,
    env,
    site,
    ket,
    terms,
    weight,
    sizes,
    joined,
    bra,
    half,
    send,
    keep,
    recv,
    mate_send,
    mate_recv,
    final,
    load_sem,
    site_send_sem,
    site_recv_sem,
    part_send_sem,
    part_recv_sem,
    mate_send_sem,
    mate_recv_sem,
    out_send_sem,
    out_recv_sem,
    edge_sem,
):
    columns, width = env.shape[1], env.shape[2]
    degree = site.shape[2]
    term_count = terms.shape[3] // 2
    chunks = columns // CHUNK
    g, c = lax.axis_index("site"), lax.axis_index("sector")
    core = lax.rem(g, 2)
    other = 1 - c
    inner = (g > 0) & (g < sites - 1)
    edge = jnp.logical_not(inner)
    mate = g + 1 - 2 * core
    far = lax.rem(g + 2 * core - 1 + sites, sites)

    loads = []
    for side, refs in enumerate(
        (
            (left_site, left_env, left_sizes, left_ket, left_terms, left_weight),
            (right_site, right_env, right_sizes, right_ket, right_terms, right_weight),
        )
    ):
        site_in, env_in, sizes_in, ket_in, terms_in, weight_in = refs
        for source, target in (
            (site_in.at[0, 0], site.at[side, c]),
            (sizes_in.at[0], sizes.at[side]),
            (env_in.at[0, 0], env.at[side]),
            (ket_in.at[0], ket.at[side]),
            (terms_in.at[0], terms.at[side]),
            (weight_in.at[0], weight.at[side]),
        ):
            loads.append(pltpu.make_async_copy(source, target, load_sem.at[len(loads)]))
    far_count = jnp.where(inner, 1, 0)
    barrier = pltpu.get_barrier_semaphore()

    def greet(peer):
        pl.semaphore_signal(barrier, inc=1, device_id=peer, device_id_type=MESH)

    greet((g, other))
    per_side = len(loads) // 2
    for i in range(per_side):
        loads[i].start()
        loads[per_side + i].start()
    pl.semaphore_wait(barrier, jnp.where(core == 1, 1, 3 + far_count))
    loads[0].wait()
    loads[per_side].wait()

    def side_of(phase):
        return 1 - core if phase == 0 else core

    def site_copy(side, owner):
        return pltpu.make_async_remote_copy(
            src_ref=site.at[side, owner],
            dst_ref=site.at[side, owner],
            send_sem=site_send_sem.at[side],
            recv_sem=site_recv_sem.at[side],
            device_id=(g, other),
            device_id_type=MESH,
        )

    def chunk_copy(source, target, send_sems, recv_sems, chunk, device):
        blocks = pl.ds(chunk * CHUNK, CHUNK)
        return pltpu.make_async_remote_copy(
            src_ref=source.at[blocks],
            dst_ref=target.at[blocks],
            send_sem=send_sems.at[chunk],
            recv_sem=recv_sems.at[chunk],
            device_id=device,
            device_id_type=MESH,
        )

    def part_copy(phase, chunk):
        return chunk_copy(
            send.at[phase],
            recv.at[phase],
            part_send_sem.at[phase],
            part_recv_sem.at[phase],
            chunk,
            (g if phase == 0 else mate, other),
        )

    def mate_copy(chunk):
        return chunk_copy(mate_send, mate_recv, mate_send_sem, mate_recv_sem, chunk, (mate, c))

    def out_copy(chunk, side):
        return chunk_copy(final, out.at[side], out_send_sem, out_recv_sem, chunk, (far, other))

    for phase in range(2):
        site_copy(side_of(phase), c).start()
    greet((mate, c))
    greet((mate, other))

    @pl.when(inner)
    def _():
        greet((far, other))


    def await_loads(first, last):
        for i in range(first, last):
            loads[i].wait()
            loads[per_side + i].wait()

    await_loads(1, 2)
    edge_copy = pltpu.make_async_copy(env.at[core], out.at[core], edge_sem)

    row = lax.broadcasted_iota(jnp.int32, (width, width), 0)

    def prepare(side, a):
        inside = row < sizes[side, a]
        for s in range(degree):
            block = jnp.where(inside, site[side, a, s].astype(jnp.float32), 0.0)
            joined[side, a, :, s * width : (s + 1) * width] = block.astype(jnp.bfloat16)
            bra[side, a * degree + s] = block.T

    def fill_half(side):
        def step(i, carry):
            rows = []
            for b in range(HALF_STEP):
                v = i * HALF_STEP + b
                block = env[side, v]
                second = ket[side, c, v].astype(jnp.float32).astype(jnp.bfloat16)
                first = (1 - ket[side, c, v]).astype(jnp.float32).astype(jnp.bfloat16)
                rows.append(jnp.concatenate([block * first, block * second], axis=1))
            both = jnp.concatenate([joined[side, 0], joined[side, 1]], axis=0)
            table = jnp.dot(
                jnp.concatenate(rows, axis=0), both, preferred_element_type=jnp.float32
            ).astype(jnp.bfloat16)
            for b in range(HALF_STEP):
                for t in range(degree):
                    half[side, (i * HALF_STEP + b) * degree + t] = table[
                        b * width : (b + 1) * width, t * width : (t + 1) * width
                    ]
            return carry

        lax.fori_loop(0, columns // HALF_STEP, step, 0)

    def partial_sum(side, k, w):
        bras, halves = [], []
        for j in range(term_count):
            f = c * term_count + j
            v = jnp.maximum(terms[side, 0, k, f, w] - c * columns, 0)
            t = terms[side, 1, k, f, w]
            u = terms[side, 2, k, f, w]
            bras.append((bra[side, u] * weight[side, k, f, w]).astype(jnp.bfloat16))
            halves.append(half[side, v * degree + t])
        return jnp.dot(
            jnp.concatenate(bras, axis=1),
            jnp.concatenate(halves, axis=0),
            preferred_element_type=jnp.float32,
        )

    far_side, mate_side = side_of(0), side_of(1)

    def send_chunk(phase, chunk):
        for b in range(CHUNK):
            w = chunk * CHUNK + b
            sector = c if phase == 0 else other
            send[phase, w] = partial_sum(side_of(phase), sector, w).astype(jnp.bfloat16)
        part_copy(phase, chunk).start()

    def far_send_step(chunk, carry):
        send_chunk(0, chunk)
        return carry

    def far_keep_step(w, carry):
        keep[w] = partial_sum(far_side, other, w)
        return carry

    def mate_send_step(chunk, carry):
        send_chunk(1, chunk)
        part_copy(0, chunk).wait_recv()
        for b in range(CHUNK):
            w = chunk * CHUNK + b
            final[w] = (keep[w] + recv[0, w].astype(jnp.float32)).astype(jnp.bfloat16)

        @pl.when(inner)
        def _():
            out_copy(chunk, far_side).start()

        return carry

    def mate_keep_step(chunk, carry):
        for b in range(CHUNK):
            w = chunk * CHUNK + b
            mate_send[w] = partial_sum(mate_side, c, w).astype(jnp.bfloat16)
        mate_copy(chunk).start()
        return carry

    def mate_add_step(chunk, carry):
        mate_copy(chunk).wait()
        part_copy(0, chunk).wait_send()

        @pl.when(inner)
        def _():
            out_copy(chunk, mate_side).wait()

        part_copy(1, chunk).wait()
        for b in range(CHUNK):
            w = chunk * CHUNK + b
            total = mate_recv[w].astype(jnp.float32) + recv[1, w].astype(jnp.float32)
            out[far_side, w] = total.astype(jnp.bfloat16)
        return carry

    prepare(far_side, c)
    prepare(mate_side, c)
    await_loads(2, 4)
    site_copy(far_side, other).wait_recv()
    prepare(far_side, other)
    fill_half(far_side)
    await_loads(4, per_side)
    lax.fori_loop(0, chunks, far_send_step, 0)

    @pl.when(edge)
    def _():
        edge_copy.start()

    lax.fori_loop(0, columns, far_keep_step, 0)
    site_copy(mate_side, other).wait_recv()
    prepare(mate_side, other)
    fill_half(mate_side)

    @pl.when(core == 1)
    def _():
        pl.semaphore_wait(barrier, 2 + far_count)

    lax.fori_loop(0, chunks, mate_send_step, 0)
    lax.fori_loop(0, chunks, mate_keep_step, 0)

    @pl.when(edge)
    def _():
        edge_copy.wait()

    for phase in range(2):
        site_copy(side_of(phase), c).wait_send()
    lax.fori_loop(0, chunks, mate_add_step, 0)

def on_device(*args):
    args = args[:6] + tuple(jnp.swapaxes(table, -1, -2) for table in args[6:10]) + args[10:]
    left_env, left_site, left_ket, left_terms = args[0], args[2], args[4], args[6]
    columns, width = left_env.shape[2], left_env.shape[3]
    degree = left_site.shape[2]
    chunks = columns // CHUNK
    blocks = (columns, width, width)
    bf16, f32 = jnp.bfloat16, jnp.float32
    sites = lax.axis_size("site")
    out = pl.pallas_call(
        functools.partial(kernel, sites),
        out_shape=jax.ShapeDtypeStruct((2,) + blocks, bf16),
        in_specs=[pl.BlockSpec(memory_space=pltpu.HBM)] * len(args),
        out_specs=pl.BlockSpec(memory_space=pltpu.VMEM),
        scratch_shapes=[
            pltpu.VMEM((2,) + blocks, bf16),
            pltpu.VMEM((2, 2, degree, width, width), bf16),
            pltpu.SMEM((2,) + left_ket.shape[1:], jnp.int32),
            pltpu.SMEM((2,) + left_terms.shape[1:], jnp.int32),
            pltpu.SMEM((2,) + left_terms.shape[2:], f32),
            pltpu.SMEM((2, 2), jnp.int32),
            pltpu.VMEM((2, 2, width, degree * width), bf16),
            pltpu.VMEM((2, 2 * degree, width, width), f32),
            pltpu.VMEM((2, columns * degree, width, width), bf16),
            pltpu.VMEM((2,) + blocks, bf16),
            pltpu.VMEM(blocks, f32),
            pltpu.VMEM((2,) + blocks, bf16),
            pltpu.VMEM(blocks, bf16),
            pltpu.VMEM(blocks, bf16),
            pltpu.VMEM(blocks, bf16),
            pltpu.SemaphoreType.DMA((len(args),)),
            pltpu.SemaphoreType.DMA((2,)),
            pltpu.SemaphoreType.DMA((2,)),
            pltpu.SemaphoreType.DMA((2, chunks)),
            pltpu.SemaphoreType.DMA((2, chunks)),
            pltpu.SemaphoreType.DMA((chunks,)),
            pltpu.SemaphoreType.DMA((chunks,)),
            pltpu.SemaphoreType.DMA((chunks,)),
            pltpu.SemaphoreType.DMA((chunks,)),
            pltpu.SemaphoreType.DMA,
        ],
        compiler_params=pltpu.CompilerParams(
            collective_id=0, has_side_effects=True, vmem_limit_bytes=40 * 1024 * 1024
        ),
    )(*[pltpu.with_memory_space_constraint(a, pltpu.HBM) for a in args])
    return out[0][None, None], out[1][None, None]


def solution(mesh):
    blocks = P("site", "sector", None, None, None)
    return jax.shard_map(
        on_device,
        mesh=mesh,
        in_specs=(
            blocks,
            blocks,
            blocks,
            blocks,
            P("site", None, None),
            P("site", None, None),
            P("site", None, None, None, None),
            P("site", None, None, None, None),
            P("site", None, None, None),
            P("site", None, None, None),
            P("site", None),
            P("site", None),
        ),
        out_specs=(blocks, blocks),
        check_vma=False,
    )
```

```python
import functools

import jax
import jax.numpy as jnp
from jax import lax
from jax.experimental import pallas as pl
from jax.experimental.pallas import tpu as pltpu
from jax.sharding import PartitionSpec as P

MESH = pl.DeviceIdType.MESH
CHUNK = 5
HALF_STEP = 10


def kernel(
    sites,
    left_env,
    right_env,
    left_site,
    right_site,
    left_ket,
    right_ket,
    left_terms,
    right_terms,
    left_weight,
    right_weight,
    left_sizes,
    right_sizes,
    out,
    env,
    site,
    ket,
    terms,
    weight,
    sizes,
    joined,
    bra,
    half,
    send,
    keep,
    recv,
    mate_send,
    mate_recv,
    final,
    load_sem,
    site_send_sem,
    site_recv_sem,
    part_send_sem,
    part_recv_sem,
    mate_send_sem,
    mate_recv_sem,
    out_send_sem,
    out_recv_sem,
    edge_sem,
    answer_sem,
):
    columns, width = env.shape[1], env.shape[2]
    degree = site.shape[2]
    term_count = terms.shape[3] // 2
    chunks = columns // CHUNK
    g, c = lax.axis_index("site"), lax.axis_index("sector")
    core = lax.rem(g, 2)
    other = 1 - c
    inner = (g > 0) & (g < sites - 1)
    edge = jnp.logical_not(inner)
    mate = g + 1 - 2 * core
    far = lax.rem(g + 2 * core - 1 + sites, sites)

    loads = []
    for side, refs in enumerate(
        (
            (left_site, left_env, left_sizes, left_ket, left_terms, left_weight),
            (right_site, right_env, right_sizes, right_ket, right_terms, right_weight),
        )
    ):
        site_in, env_in, sizes_in, ket_in, terms_in, weight_in = refs
        for source, target in (
            (site_in.at[0, 0], site.at[side, c]),
            (sizes_in.at[0], sizes.at[side]),
            (env_in.at[0, 0], env.at[side]),
            (ket_in.at[0], ket.at[side]),
            (terms_in.at[0], terms.at[side]),
            (weight_in.at[0], weight.at[side]),
        ):
            loads.append(pltpu.make_async_copy(source, target, load_sem.at[len(loads)]))
    far_count = jnp.where(inner, 1, 0)
    barrier = pltpu.get_barrier_semaphore()

    def greet(sem):
        @pl.when(inner)
        def _():
            pl.semaphore_signal(sem, inc=1, device_id=(far, other), device_id_type=MESH)

        for peer in ((mate, c), (mate, other)):
            pl.semaphore_signal(sem, inc=1, device_id=peer, device_id_type=MESH)

    pl.semaphore_signal(barrier, inc=1, device_id=(g, other), device_id_type=MESH)

    @pl.when(core == 1)
    def _():
        greet(barrier)

    per_side = len(loads) // 2
    for i in range(per_side):
        loads[i].start()
        loads[per_side + i].start()
    pl.semaphore_wait(barrier, jnp.where(core == 1, 1, 3 + far_count))
    loads[0].wait()
    loads[per_side].wait()

    def side_of(phase):
        return 1 - core if phase == 0 else core

    def site_copy(side, owner):
        return pltpu.make_async_remote_copy(
            src_ref=site.at[side, owner],
            dst_ref=site.at[side, owner],
            send_sem=site_send_sem.at[side],
            recv_sem=site_recv_sem.at[side],
            device_id=(g, other),
            device_id_type=MESH,
        )

    def chunk_copy(source, target, send_sems, recv_sems, chunk, device):
        blocks = pl.ds(chunk * CHUNK, CHUNK)
        return pltpu.make_async_remote_copy(
            src_ref=source.at[blocks],
            dst_ref=target.at[blocks],
            send_sem=send_sems.at[chunk],
            recv_sem=recv_sems.at[chunk],
            device_id=device,
            device_id_type=MESH,
        )

    def part_copy(phase, chunk):
        return chunk_copy(
            send.at[phase],
            recv.at[phase],
            part_send_sem.at[phase],
            part_recv_sem.at[phase],
            chunk,
            (g if phase == 0 else mate, other),
        )

    def mate_copy(chunk):
        return chunk_copy(mate_send, mate_recv, mate_send_sem, mate_recv_sem, chunk, (mate, c))

    def out_copy(chunk, side):
        return chunk_copy(final, out.at[side], out_send_sem, out_recv_sem, chunk, (far, other))

    for phase in range(2):
        site_copy(side_of(phase), c).start()

    @pl.when(core == 0)
    def _():
        greet(answer_sem)


    def await_loads(first, last):
        for i in range(first, last):
            loads[i].wait()
            loads[per_side + i].wait()

    await_loads(1, 2)
    edge_copy = pltpu.make_async_copy(env.at[core], out.at[core], edge_sem)

    row = lax.broadcasted_iota(jnp.int32, (width, width), 0)

    def prepare(side, a):
        inside = row < sizes[side, a]
        for s in range(degree):
            block = jnp.where(inside, site[side, a, s].astype(jnp.float32), 0.0)
            joined[side, a, :, s * width : (s + 1) * width] = block.astype(jnp.bfloat16)
            bra[side, a * degree + s] = block.T

    def fill_half(side):
        def step(i, carry):
            rows = []
            for b in range(HALF_STEP):
                v = i * HALF_STEP + b
                block = env[side, v]
                second = ket[side, c, v].astype(jnp.float32).astype(jnp.bfloat16)
                first = (1 - ket[side, c, v]).astype(jnp.float32).astype(jnp.bfloat16)
                rows.append(jnp.concatenate([block * first, block * second], axis=1))
            both = jnp.concatenate([joined[side, 0], joined[side, 1]], axis=0)
            table = jnp.dot(
                jnp.concatenate(rows, axis=0), both, preferred_element_type=jnp.float32
            ).astype(jnp.bfloat16)
            for b in range(HALF_STEP):
                for t in range(degree):
                    half[side, (i * HALF_STEP + b) * degree + t] = table[
                        b * width : (b + 1) * width, t * width : (t + 1) * width
                    ]
            return carry

        lax.fori_loop(0, columns // HALF_STEP, step, 0)

    def partial_sum(side, k, w):
        bras, halves = [], []
        for j in range(term_count):
            f = c * term_count + j
            v = jnp.maximum(terms[side, 0, k, f, w] - c * columns, 0)
            t = terms[side, 1, k, f, w]
            u = terms[side, 2, k, f, w]
            bras.append((bra[side, u] * weight[side, k, f, w]).astype(jnp.bfloat16))
            halves.append(half[side, v * degree + t])
        return jnp.dot(
            jnp.concatenate(bras, axis=1),
            jnp.concatenate(halves, axis=0),
            preferred_element_type=jnp.float32,
        )

    far_side, mate_side = side_of(0), side_of(1)

    def send_chunk(phase, chunk):
        for b in range(CHUNK):
            w = chunk * CHUNK + b
            sector = c if phase == 0 else other
            send[phase, w] = partial_sum(side_of(phase), sector, w).astype(jnp.bfloat16)
        part_copy(phase, chunk).start()

    def far_send_step(chunk, carry):
        send_chunk(0, chunk)
        return carry

    def far_keep_step(w, carry):
        keep[w] = partial_sum(far_side, other, w)
        return carry

    def mate_send_step(chunk, carry):
        send_chunk(1, chunk)
        part_copy(0, chunk).wait_recv()
        for b in range(CHUNK):
            w = chunk * CHUNK + b
            final[w] = (keep[w] + recv[0, w].astype(jnp.float32)).astype(jnp.bfloat16)

        @pl.when(inner)
        def _():
            out_copy(chunk, far_side).start()

        return carry

    def mate_keep_step(chunk, carry):
        for b in range(CHUNK):
            w = chunk * CHUNK + b
            mate_send[w] = partial_sum(mate_side, c, w).astype(jnp.bfloat16)
        mate_copy(chunk).start()
        return carry

    def mate_add_step(chunk, carry):
        mate_copy(chunk).wait()
        part_copy(0, chunk).wait_send()

        @pl.when(inner)
        def _():
            out_copy(chunk, mate_side).wait()

        part_copy(1, chunk).wait()
        for b in range(CHUNK):
            w = chunk * CHUNK + b
            total = mate_recv[w].astype(jnp.float32) + recv[1, w].astype(jnp.float32)
            out[far_side, w] = total.astype(jnp.bfloat16)
        return carry

    prepare(far_side, c)
    prepare(mate_side, c)
    await_loads(2, 4)
    site_copy(far_side, other).wait_recv()
    prepare(far_side, other)
    fill_half(far_side)
    await_loads(4, per_side)
    lax.fori_loop(0, chunks, far_send_step, 0)

    @pl.when(edge)
    def _():
        edge_copy.start()

    lax.fori_loop(0, columns, far_keep_step, 0)
    site_copy(mate_side, other).wait_recv()
    prepare(mate_side, other)
    fill_half(mate_side)

    @pl.when(core == 1)
    def _():
        pl.semaphore_wait(answer_sem, 2 + far_count)

    lax.fori_loop(0, chunks, mate_send_step, 0)
    lax.fori_loop(0, chunks, mate_keep_step, 0)

    @pl.when(edge)
    def _():
        edge_copy.wait()

    for phase in range(2):
        site_copy(side_of(phase), c).wait_send()
    lax.fori_loop(0, chunks, mate_add_step, 0)

def on_device(*args):
    args = args[:6] + tuple(jnp.swapaxes(table, -1, -2) for table in args[6:10]) + args[10:]
    left_env, left_site, left_ket, left_terms = args[0], args[2], args[4], args[6]
    columns, width = left_env.shape[2], left_env.shape[3]
    degree = left_site.shape[2]
    chunks = columns // CHUNK
    blocks = (columns, width, width)
    bf16, f32 = jnp.bfloat16, jnp.float32
    sites = lax.axis_size("site")
    out = pl.pallas_call(
        functools.partial(kernel, sites),
        out_shape=jax.ShapeDtypeStruct((2,) + blocks, bf16),
        in_specs=[pl.BlockSpec(memory_space=pltpu.HBM)] * len(args),
        out_specs=pl.BlockSpec(memory_space=pltpu.VMEM),
        scratch_shapes=[
            pltpu.VMEM((2,) + blocks, bf16),
            pltpu.VMEM((2, 2, degree, width, width), bf16),
            pltpu.SMEM((2,) + left_ket.shape[1:], jnp.int32),
            pltpu.SMEM((2,) + left_terms.shape[1:], jnp.int32),
            pltpu.SMEM((2,) + left_terms.shape[2:], f32),
            pltpu.SMEM((2, 2), jnp.int32),
            pltpu.VMEM((2, 2, width, degree * width), bf16),
            pltpu.VMEM((2, 2 * degree, width, width), f32),
            pltpu.VMEM((2, columns * degree, width, width), bf16),
            pltpu.VMEM((2,) + blocks, bf16),
            pltpu.VMEM(blocks, f32),
            pltpu.VMEM((2,) + blocks, bf16),
            pltpu.VMEM(blocks, bf16),
            pltpu.VMEM(blocks, bf16),
            pltpu.VMEM(blocks, bf16),
            pltpu.SemaphoreType.DMA((len(args),)),
            pltpu.SemaphoreType.DMA((2,)),
            pltpu.SemaphoreType.DMA((2,)),
            pltpu.SemaphoreType.DMA((2, chunks)),
            pltpu.SemaphoreType.DMA((2, chunks)),
            pltpu.SemaphoreType.DMA((chunks,)),
            pltpu.SemaphoreType.DMA((chunks,)),
            pltpu.SemaphoreType.DMA((chunks,)),
            pltpu.SemaphoreType.DMA((chunks,)),
            pltpu.SemaphoreType.DMA,
            pltpu.SemaphoreType.REGULAR,
        ],
        compiler_params=pltpu.CompilerParams(
            collective_id=0, has_side_effects=True, vmem_limit_bytes=40 * 1024 * 1024
        ),
    )(*[pltpu.with_memory_space_constraint(a, pltpu.HBM) for a in args])
    return out[0][None, None], out[1][None, None]


def solution(mesh):
    blocks = P("site", "sector", None, None, None)
    return jax.shard_map(
        on_device,
        mesh=mesh,
        in_specs=(
            blocks,
            blocks,
            blocks,
            blocks,
            P("site", None, None),
            P("site", None, None),
            P("site", None, None, None, None),
            P("site", None, None, None, None),
            P("site", None, None, None),
            P("site", None, None, None),
            P("site", None),
            P("site", None),
        ),
        out_specs=(blocks, blocks),
        check_vma=False,
    )
```

```python
import functools

import jax
import jax.numpy as jnp
from jax import lax
from jax.experimental import pallas as pl
from jax.experimental.pallas import tpu as pltpu
from jax.sharding import PartitionSpec as P

MESH = pl.DeviceIdType.MESH
HEAD, CHUNK, TAIL = (2,), 6, (4,)
HALF_STEP = 15


def kernel(
    sites,
    left_env,
    right_env,
    left_site,
    right_site,
    left_ket,
    right_ket,
    left_terms,
    right_terms,
    left_weight,
    right_weight,
    left_sizes,
    right_sizes,
    out,
    env,
    site,
    ket,
    terms,
    weight,
    sizes,
    joined,
    bra,
    half,
    send,
    keep,
    recv,
    mate_send,
    mate_recv,
    final,
    load_sem,
    site_send_sem,
    site_recv_sem,
    part_send_sem,
    part_recv_sem,
    mate_send_sem,
    mate_recv_sem,
    out_send_sem,
    out_recv_sem,
    edge_sem,
    answer_sem,
):
    columns, width = env.shape[1], env.shape[2]
    degree = site.shape[2]
    term_count = terms.shape[3] // 2
    middle = (columns - sum(HEAD) - sum(TAIL)) // CHUNK
    g, c = lax.axis_index("site"), lax.axis_index("sector")
    core = lax.rem(g, 2)
    other = 1 - c
    inner = (g > 0) & (g < sites - 1)
    edge = jnp.logical_not(inner)
    mate = g + 1 - 2 * core
    far = lax.rem(g + 2 * core - 1 + sites, sites)

    loads = []
    for side, refs in enumerate(
        (
            (left_site, left_env, left_sizes, left_ket, left_terms, left_weight),
            (right_site, right_env, right_sizes, right_ket, right_terms, right_weight),
        )
    ):
        site_in, env_in, sizes_in, ket_in, terms_in, weight_in = refs
        for source, target in (
            (site_in.at[0, 0], site.at[side, c]),
            (sizes_in.at[0], sizes.at[side]),
            (env_in.at[0, 0], env.at[side]),
            (ket_in.at[0], ket.at[side]),
            (terms_in.at[0], terms.at[side]),
            (weight_in.at[0], weight.at[side]),
        ):
            loads.append(pltpu.make_async_copy(source, target, load_sem.at[len(loads)]))
    far_count = jnp.where(inner, 1, 0)
    barrier = pltpu.get_barrier_semaphore()

    def greet(sem):
        @pl.when(inner)
        def _():
            pl.semaphore_signal(sem, inc=1, device_id=(far, other), device_id_type=MESH)

        for peer in ((mate, c), (mate, other)):
            pl.semaphore_signal(sem, inc=1, device_id=peer, device_id_type=MESH)

    pl.semaphore_signal(barrier, inc=1, device_id=(g, other), device_id_type=MESH)

    @pl.when(core == 1)
    def _():
        greet(barrier)

    per_side = len(loads) // 2
    for i in range(per_side):
        loads[i].start()
        loads[per_side + i].start()
    pl.semaphore_wait(barrier, jnp.where(core == 1, 1, 3 + far_count))
    loads[0].wait()
    loads[per_side].wait()

    def side_of(phase):
        return 1 - core if phase == 0 else core

    def site_copy(side, owner):
        return pltpu.make_async_remote_copy(
            src_ref=site.at[side, owner],
            dst_ref=site.at[side, owner],
            send_sem=site_send_sem.at[side],
            recv_sem=site_recv_sem.at[side],
            device_id=(g, other),
            device_id_type=MESH,
        )

    def each_chunk(step):
        first = 0
        for i, size in enumerate(HEAD):
            step(i, first, size)
            first += size

        def one(i, carry):
            step(len(HEAD) + i, first + i * CHUNK, CHUNK)
            return carry

        lax.fori_loop(0, middle, one, 0)
        last = first + middle * CHUNK
        for i, size in enumerate(TAIL):
            step(len(HEAD) + middle + i, last, size)
            last += size

    def chunk_copy(source, target, send_sems, recv_sems, chunk, device):
        index, first, size = chunk
        blocks = pl.ds(first, size)
        return pltpu.make_async_remote_copy(
            src_ref=source.at[blocks],
            dst_ref=target.at[blocks],
            send_sem=send_sems.at[index],
            recv_sem=recv_sems.at[index],
            device_id=device,
            device_id_type=MESH,
        )

    def part_copy(phase, chunk):
        return chunk_copy(
            send.at[phase],
            recv.at[phase],
            part_send_sem.at[phase],
            part_recv_sem.at[phase],
            chunk,
            (g if phase == 0 else mate, other),
        )

    def mate_copy(chunk):
        return chunk_copy(mate_send, mate_recv, mate_send_sem, mate_recv_sem, chunk, (mate, c))

    def out_copy(chunk, side):
        return chunk_copy(final, out.at[side], out_send_sem, out_recv_sem, chunk, (far, other))

    for phase in range(2):
        site_copy(side_of(phase), c).start()

    @pl.when(core == 0)
    def _():
        greet(answer_sem)


    def await_loads(first, last):
        for i in range(first, last):
            loads[i].wait()
            loads[per_side + i].wait()

    await_loads(1, 2)
    edge_copy = pltpu.make_async_copy(env.at[core], out.at[core], edge_sem)

    row = lax.broadcasted_iota(jnp.int32, (width, width), 0)

    def prepare(side, a):
        inside = row < sizes[side, a]
        for s in range(degree):
            block = jnp.where(inside, site[side, a, s].astype(jnp.float32), 0.0)
            joined[side, a, :, s * width : (s + 1) * width] = block.astype(jnp.bfloat16)
            bra[side, a * degree + s] = block.T

    def fill_half(side):
        def step(i, carry):
            rows = []
            for b in range(HALF_STEP):
                v = i * HALF_STEP + b
                block = env[side, v]
                second = ket[side, c, v].astype(jnp.float32).astype(jnp.bfloat16)
                first = (1 - ket[side, c, v]).astype(jnp.float32).astype(jnp.bfloat16)
                rows.append(jnp.concatenate([block * first, block * second], axis=1))
            both = jnp.concatenate([joined[side, 0], joined[side, 1]], axis=0)
            table = jnp.dot(
                jnp.concatenate(rows, axis=0), both, preferred_element_type=jnp.float32
            ).astype(jnp.bfloat16)
            for b in range(HALF_STEP):
                for t in range(degree):
                    half[side, (i * HALF_STEP + b) * degree + t] = table[
                        b * width : (b + 1) * width, t * width : (t + 1) * width
                    ]
            return carry

        lax.fori_loop(0, columns // HALF_STEP, step, 0)

    def partial_sum(side, k, w):
        bras, halves = [], []
        for j in range(term_count):
            f = c * term_count + j
            v = jnp.maximum(terms[side, 0, k, f, w] - c * columns, 0)
            t = terms[side, 1, k, f, w]
            u = terms[side, 2, k, f, w]
            bras.append((bra[side, u] * weight[side, k, f, w]).astype(jnp.bfloat16))
            halves.append(half[side, v * degree + t])
        return jnp.dot(
            jnp.concatenate(bras, axis=1),
            jnp.concatenate(halves, axis=0),
            preferred_element_type=jnp.float32,
        )

    far_side, mate_side = side_of(0), side_of(1)

    def send_chunk(phase, chunk):
        for b in range(chunk[2]):
            w = chunk[1] + b
            sector = c if phase == 0 else other
            send[phase, w] = partial_sum(side_of(phase), sector, w).astype(jnp.bfloat16)
        part_copy(phase, chunk).start()

    def far_send_step(*chunk):
        send_chunk(0, chunk)

    def far_keep_step(w, carry):
        keep[w] = partial_sum(far_side, other, w)
        return carry

    def mate_send_step(*chunk):
        send_chunk(1, chunk)
        part_copy(0, chunk).wait_recv()
        for b in range(chunk[2]):
            w = chunk[1] + b
            final[w] = (keep[w] + recv[0, w].astype(jnp.float32)).astype(jnp.bfloat16)

        @pl.when(inner)
        def _():
            out_copy(chunk, far_side).start()

    def mate_keep_step(*chunk):
        for b in range(chunk[2]):
            w = chunk[1] + b
            mate_send[w] = partial_sum(mate_side, c, w).astype(jnp.bfloat16)
        mate_copy(chunk).start()

    def mate_add_step(*chunk):
        mate_copy(chunk).wait()
        part_copy(0, chunk).wait_send()

        @pl.when(inner)
        def _():
            out_copy(chunk, mate_side).wait()

        part_copy(1, chunk).wait()
        for b in range(chunk[2]):
            w = chunk[1] + b
            total = mate_recv[w].astype(jnp.float32) + recv[1, w].astype(jnp.float32)
            out[far_side, w] = total.astype(jnp.bfloat16)

    prepare(far_side, c)
    prepare(mate_side, c)
    await_loads(2, 4)
    site_copy(far_side, other).wait_recv()
    prepare(far_side, other)
    fill_half(far_side)
    await_loads(4, per_side)
    each_chunk(far_send_step)

    @pl.when(edge)
    def _():
        edge_copy.start()

    lax.fori_loop(0, columns, far_keep_step, 0)
    site_copy(mate_side, other).wait_recv()
    prepare(mate_side, other)
    fill_half(mate_side)

    @pl.when(core == 1)
    def _():
        pl.semaphore_wait(answer_sem, 2 + far_count)

    each_chunk(mate_send_step)
    each_chunk(mate_keep_step)

    @pl.when(edge)
    def _():
        edge_copy.wait()

    for phase in range(2):
        site_copy(side_of(phase), c).wait_send()
    each_chunk(mate_add_step)

def on_device(*args):
    args = args[:6] + tuple(jnp.swapaxes(table, -1, -2) for table in args[6:10]) + args[10:]
    left_env, left_site, left_ket, left_terms = args[0], args[2], args[4], args[6]
    columns, width = left_env.shape[2], left_env.shape[3]
    degree = left_site.shape[2]
    chunks = len(HEAD) + (columns - sum(HEAD) - sum(TAIL)) // CHUNK + len(TAIL)
    blocks = (columns, width, width)
    bf16, f32 = jnp.bfloat16, jnp.float32
    sites = lax.axis_size("site")
    out = pl.pallas_call(
        functools.partial(kernel, sites),
        out_shape=jax.ShapeDtypeStruct((2,) + blocks, bf16),
        in_specs=[pl.BlockSpec(memory_space=pltpu.HBM)] * len(args),
        out_specs=pl.BlockSpec(memory_space=pltpu.VMEM),
        scratch_shapes=[
            pltpu.VMEM((2,) + blocks, bf16),
            pltpu.VMEM((2, 2, degree, width, width), bf16),
            pltpu.SMEM((2,) + left_ket.shape[1:], jnp.int32),
            pltpu.SMEM((2,) + left_terms.shape[1:], jnp.int32),
            pltpu.SMEM((2,) + left_terms.shape[2:], f32),
            pltpu.SMEM((2, 2), jnp.int32),
            pltpu.VMEM((2, 2, width, degree * width), bf16),
            pltpu.VMEM((2, 2 * degree, width, width), f32),
            pltpu.VMEM((2, columns * degree, width, width), bf16),
            pltpu.VMEM((2,) + blocks, bf16),
            pltpu.VMEM(blocks, f32),
            pltpu.VMEM((2,) + blocks, bf16),
            pltpu.VMEM(blocks, bf16),
            pltpu.VMEM(blocks, bf16),
            pltpu.VMEM(blocks, bf16),
            pltpu.SemaphoreType.DMA((len(args),)),
            pltpu.SemaphoreType.DMA((2,)),
            pltpu.SemaphoreType.DMA((2,)),
            pltpu.SemaphoreType.DMA((2, chunks)),
            pltpu.SemaphoreType.DMA((2, chunks)),
            pltpu.SemaphoreType.DMA((chunks,)),
            pltpu.SemaphoreType.DMA((chunks,)),
            pltpu.SemaphoreType.DMA((chunks,)),
            pltpu.SemaphoreType.DMA((chunks,)),
            pltpu.SemaphoreType.DMA,
            pltpu.SemaphoreType.REGULAR,
        ],
        compiler_params=pltpu.CompilerParams(
            collective_id=0, has_side_effects=True, vmem_limit_bytes=40 * 1024 * 1024
        ),
    )(*[pltpu.with_memory_space_constraint(a, pltpu.HBM) for a in args])
    return out[0][None, None], out[1][None, None]


def solution(mesh):
    blocks = P("site", "sector", None, None, None)
    return jax.shard_map(
        on_device,
        mesh=mesh,
        in_specs=(
            blocks,
            blocks,
            blocks,
            blocks,
            P("site", None, None),
            P("site", None, None),
            P("site", None, None, None, None),
            P("site", None, None, None, None),
            P("site", None, None, None),
            P("site", None, None, None),
            P("site", None),
            P("site", None),
        ),
        out_specs=(blocks, blocks),
        check_vma=False,
    )
```
